32 devices in a mesh: seq: 8 (over y, x, core), grp: 4 (over z).
Axes of the slice: x: 2, y: 2, z: 4, core: 2. Of those that a mesh axis runs over, the one named last changes fastest.
Arguments:
- inputs: bfloat16 [4, 8192, 384], P('grp', 'seq'), may hold values from -6 to 6
- segment: int32 [4, 8192], P('grp', 'seq'), may hold values from 0 to 3, never falling along the last dimension, each value on 1 to 4096 neighbouring positions
- conv_weight: bfloat16 [5, 384, 384], P(None, 'grp'), may hold values from -0.125 to 0.125
- proj_weight: bfloat16 [384, 448], P('grp'), may hold values from -0.3125 to 0.3125
- cotangent: bfloat16 [4, 4096, 448], P('grp', 'seq'), may hold values from -6 to 6
Outputs:
- pooled_out: bfloat16 [4, 4096, 448], P('grp', 'seq')
- input_grad: bfloat16 [4, 8192, 384], P('grp', 'seq')
- conv_grad: float32 [5, 384, 384], P(None, 'grp', 'seq')
- proj_grad: float32 [384, 448], P('grp', 'seq')
The draws below stay inside these ranges and needn't reach their ends.
Inputs may be any that keep to these rules, and one draw needn't show every extreme that they name: `segment`: along each window the interval numbers never fall; every interval covers 1 to 4096 positions and one covers exactly 4096.
All inputs are finite; a program needn't handle non-finite values.
Results may differ from the reference program's by a relative error of at most 0.018.
Values may be sent and summed in bfloat16 or wider, within the bound.
A program may use at most 64 MiB of HBM per device.

```python
import math
import jax
import jax.numpy as jnp
import numpy as np
from jax import lax

ROWS = 1024
C0 = 384
C1 = 448
SEQ_LEN = 8192
POOLED = 4096
BATCH = 4
N_SEQ = 8


def raised(drawn, rng, source, target, shards_of, factor):
    owner, partner = [(jnp.arange(drawn.shape[position]) // (drawn.shape[position] // shards_of)).reshape([-1 if axis == position else 1 for axis in range(drawn.ndim)]) for position in (source, target)]
    chosen = jax.random.permutation(rng, shards_of)[partner]
    strong = (owner == chosen) | (owner == (partner + shards_of // 2) % shards_of)
    return jnp.where(strong, factor * drawn, drawn)


def levels(key, shape, cuts, smallest, top_value):
    def one(dim, parts):
        draws = jax.random.uniform(jax.random.fold_in(jax.random.fold_in(key, 6), dim), (parts,), jnp.float32, smallest / len(cuts), top_value / len(cuts))
        return jnp.repeat(jnp.exp(draws), shape[dim] // parts).reshape((-1,) + (1,) * (len(shape) - dim - 1))

    gain = one(*cuts[0])
    for cut in cuts[1:]:
        gain = gain * one(*cut)
    return gain


def length_profile(count, total, limit, lean):
    weights = [(1 << 20) // math.isqrt(standing ** lean) + 1 for standing in range(2, count + 1)]
    spare, holding = total - limit - (count - 1), [1] * (count - 1)
    while spare > 0:
        movable = [i for i in range(count - 1) if holding[i] < limit]
        mass, budget = sum([weights[i] for i in movable]), spare
        for i in movable:
            extra = min(limit - holding[i], max(1, budget * weights[i] // mass), spare)
            holding[i] = holding[i] + extra
            spare = spare - extra
    return np.array([limit] + holding)


def ragged(stream_key, count, total, reach, slope):
    if count == 2:
        one = jax.random.randint(stream_key, (), max(1, total - reach), min(reach, total - 1) + 1)
        return jnp.stack([one, total - one])
    lengths = jnp.asarray(length_profile(count, total, reach, slope), jnp.int32)
    pairs = (count - 1) // 2
    donor, receiver = lengths[1:1 + 2 * pairs:2], lengths[2:2 + 2 * pairs:2]
    margin = jnp.minimum(donor - 1, reach - receiver)
    moved = jax.random.randint(jax.random.fold_in(stream_key, 1), (pairs,), 0, 1 << 20) % (margin + 1)
    lengths = lengths.at[1:1 + 2 * pairs:2].set(donor - moved).at[2:2 + 2 * pairs:2].set(receiver + moved)
    return lengths[jax.random.permutation(jax.random.fold_in(stream_key, 2), count)]


def gaussian(rng, shape, scale, bound, shards=(), kind=jnp.bfloat16):
    array = scale * jax.random.normal(rng, shape, jnp.float32)
    if shards:
        array = array * levels(rng, shape, shards, -0.22, 0.18)
    return jnp.clip(array, -bound, bound).astype(kind)


def heavy_noise(key, dims, width, most, split, heavy, dtype=jnp.bfloat16):
    array = width * jax.random.normal(key, dims, jnp.float32)
    if split:
        array = array * levels(key, dims, split, -0.22, 0.18)
    return jnp.clip(raised(array, jax.random.fold_in(key, 3), *heavy), -most, most).astype(dtype)


def setup_inputs(seed: int = 0) -> dict:
    splits = jax.random.split(jax.random.key(seed), 6)
    return {
        "inputs": gaussian(splits[0], (BATCH, SEQ_LEN, C0), 1.0, 6.0, ((0, 4), (1, 8))),
        "segment": jax.vmap(lambda own: jnp.searchsorted(jnp.cumsum(ragged(own, N_SEQ // 2, SEQ_LEN, 4 * ROWS, 1)), jnp.arange(SEQ_LEN), side="right"))(jax.random.split(splits[1], BATCH)).reshape((BATCH, SEQ_LEN)).astype(jnp.int32),
        "conv_weight": gaussian(splits[2], (5, C0, C0), (5 * C0) ** -0.5, 0.125, ((1, 4),)),
        "proj_weight": gaussian(splits[3], (C0, C1), C0 ** -0.5, 0.3125, ((0, 4),)),
        "cotangent": heavy_noise(splits[4], (BATCH, POOLED, C1), 1.0, 6.0, ((0, 4), (1, 8)), (1, 2, 8, 2.0)),
    }


def gelu_slope(normed):
    cdf = 0.5 * (1.0 + jax.scipy.special.erf(normed / math.sqrt(2.0)))
    density = jnp.exp(-0.5 * normed * normed) / math.sqrt(2.0 * math.pi)
    return cdf + normed * density

def one_window(packed, conv_weight, proj_weight):
    inputs, segment, cotangent = packed
    length = inputs.shape[0]
    wide = inputs.astype(jnp.float32)
    inverse = lax.rsqrt(lax.optimization_barrier(jnp.mean(wide * wide, axis=-1, keepdims=True)) + 1e-06)
    normed = wide * inverse
    act = jax.nn.gelu(normed, approximate=False).astype(jnp.bfloat16)
    act_pad = jnp.pad(act, ((2, 2), (0, 0)))
    seg_pad = jnp.pad(segment, (2, 2))
    masks = [(seg_pad[j:j + length] == segment)[:, None] for j in range(5)]
    zero_act = jnp.zeros((), jnp.bfloat16)
    shifted = jnp.stack([jnp.where(masks[j], act_pad[j:j + length], zero_act) for j in range(5)])
    conv_out = jnp.einsum('jrc,jcd->rd', shifted.astype(jnp.float32), conv_weight.astype(jnp.float32))
    hidden = (wide + conv_out).astype(jnp.bfloat16)
    paired = hidden.astype(jnp.float32).reshape(length // 2, 2, -1)
    pooled = ((paired[:, 0] + paired[:, 1]) * 0.5).astype(jnp.bfloat16)
    pooled_out = jnp.dot(pooled, proj_weight, preferred_element_type=jnp.float32).astype(jnp.bfloat16)
    pool_grad = jnp.dot(cotangent, proj_weight.T, preferred_element_type=jnp.float32)
    hidden_grad = jnp.repeat(pool_grad * 0.5, 2, axis=0).astype(jnp.bfloat16)
    proj_grad = jnp.dot(pooled.T, cotangent, preferred_element_type=jnp.float32)
    conv_grad = jnp.einsum('jrc,rd->jcd', shifted.astype(jnp.float32), hidden_grad.astype(jnp.float32))
    grad_pad = jnp.pad(hidden_grad, ((2, 2), (0, 0)))
    zero_grad = jnp.zeros((), jnp.bfloat16)
    back_shift = jnp.stack([jnp.where(masks[4 - k], grad_pad[4 - k:4 - k + length], zero_grad) for k in range(5)])
    act_grad = jnp.einsum('krd,kcd->rc', back_shift.astype(jnp.float32), conv_weight.astype(jnp.float32))
    norm_grad = act_grad * gelu_slope(normed)
    centred = norm_grad - normed * lax.optimization_barrier(jnp.mean(norm_grad * normed, axis=-1, keepdims=True))
    input_grad = (hidden_grad.astype(jnp.float32) + centred * inverse).astype(jnp.bfloat16)
    return (pooled_out, input_grad, conv_grad, proj_grad)

def reference(inputs, segment, conv_weight, proj_weight, cotangent):

    def apply_one(packed):
        return one_window(packed, conv_weight, proj_weight)
    pooled_out, input_grad, conv_parts, proj_parts = lax.map(apply_one, (inputs, segment, cotangent))
    return (pooled_out, input_grad, lax.optimization_barrier(jnp.sum(conv_parts, axis=0)), lax.optimization_barrier(jnp.sum(proj_parts, axis=0)))
```

```python
import functools
import math

import jax
import jax.numpy as jnp
from jax import lax
from jax.experimental import pallas as pl
from jax.experimental.pallas import tpu as pltpu
from jax.sharding import PartitionSpec as P

F32 = jnp.float32
BF16 = jnp.bfloat16
TAPS = 5
EDGE = 16
NT = (((1,), (1,)), ((), ()))


def up16(n):
    return -(-n // 16) * 16


def dot(a, b, dims=(((1,), (0,)), ((), ()))):
    return lax.dot_general(a, b, dims, preferred_element_type=F32)


def normalised(x):
    inverse = lax.rsqrt(jnp.mean(x * x, axis=-1, keepdims=True) + 1e-06)
    return x * inverse, inverse


def gate(r):
    return 0.5 * (1.0 + lax.erf(r * (1.0 / math.sqrt(2.0))))


def pick(rows, cols, first, per):
    r = lax.broadcasted_iota(jnp.int32, (rows, cols), 0)
    c = lax.broadcasted_iota(jnp.int32, (rows, cols), 1)
    return jnp.where(r // per + first == c, 1.0, 0.0)


class Sizes:
    def __init__(self, mesh, x, conv, proj, cot):
        self.n_seq, self.n_grp = mesh.shape["seq"], mesh.shape["grp"]
        self.n_chip = self.n_seq // 2
        self.rows, self.c0 = x
        self.half, self.c1 = cot
        self.cs = conv[1]
        self.gpt = -(-self.cs // 16)
        self.gpp = -(-TAPS * self.gpt // self.n_seq)
        self.ppp = -(-self.gpt // self.n_seq)
        self.dc, self.dp = self.c0 // self.n_seq, self.c1 // self.n_seq
        self.rc, self.rp = up16(self.dc), up16(self.dp)
        self.stage = BF16 if self.cs % 16 == 0 else F32


def scratch(z):
    ext = z.rows + 2 * EDGE
    V, S = pltpu.VMEM, pltpu.SemaphoreType.DMA
    shapes = dict(
        xh=V((2, EDGE, z.c0), BF16),
        ch=V((2, EDGE, z.c1), BF16),
        sh=V((2, EDGE, 128), jnp.int32),
        seg=V((ext, 128), jnp.int32),
        act=V((ext, z.c0), F32),
        slope=V((z.rows, z.c0), F32),
        grad=V((ext, z.c0), F32),
        gradt=V((z.c0, z.rows), BF16),
        shifted=V((z.rows, TAPS * z.c0), BF16),
        pooled=V((z.half, z.c0), BF16),
        wbuf=V((z.n_grp, z.n_chip, 2, 16 * z.gpp, z.c0), BF16),
        pbuf=V((z.n_grp, z.n_chip, 2, 16 * z.ppp, z.c1), BF16),
        wf=V((TAPS * z.c0, z.c0), z.stage),
        wb=V((z.c0, TAPS * z.c0), z.stage),
        pf=V((z.c0, z.c1), z.stage),
        halo_s=S((6,)),
        halo_r=S((6,)),
        gc_s=S((2, z.n_grp)),
        gc_r=S((2, z.n_grp)),
        gb_s=S((2, z.n_chip)),
        gb_r=S((2, z.n_chip)),
        ga_s=S((2,)),
        ga_r=S((2,)),
        ra_s=S((TAPS + 1,)),
        ra_r=S((TAPS + 1,)),
        rb_s=S((TAPS + 1, z.n_chip)),
        rb_r=S((TAPS + 1, z.n_chip)),
        rc_s=S((TAPS + 1, z.n_grp)),
        rc_r=S((TAPS + 1, z.n_grp)),
    )
    for name, units, r in (("c", TAPS, z.rc), ("p", 1, z.rp)):
        lanes = z.c0 // z.n_grp
        shapes.update({
            name + "_acc": V((units, z.n_chip, 2, r, z.c0), F32),
            name + "_sa": V((units, z.n_chip, r, z.c0), BF16),
            name + "_ra": V((units, z.n_chip, r, z.c0), BF16),
            name + "_kb": V((units, z.n_chip, r, z.c0), F32),
            name + "_sb": V((units, z.n_chip, r, z.c0), BF16),
            name + "_rb": V((units, z.n_chip, r, z.c0), BF16),
            name + "_kc": V((units, z.n_grp, r, lanes), F32),
            name + "_sc": V((units, z.n_grp, r, lanes), BF16),
            name + "_rc": V((units, z.n_grp, r, lanes), BF16),
        })
    return shapes


def kernel(z, names, x_ref, seg_ref, conv_ref, proj_ref, cot_ref, po_ref, ig_ref, cg_ref, pg_ref, *refs):
    m = dict(zip(names, refs))
    s, g = lax.axis_index("seq"), lax.axis_index("grp")
    chip, core = s // 2, s % 2
    sent = []

    def at(s2, g2):
        return {"seq": s2, "grp": g2}

    def turn(i, k, n):
        return lax.rem(i + k, n)

    def remote(src, dst, ss, rs, to):
        return pltpu.make_async_remote_copy(
            src_ref=src, dst_ref=dst, send_sem=ss, recv_sem=rs, device_id=to, device_id_type=pl.DeviceIdType.MESH
        )

    def go(copies):
        for c in copies:
            c.start()
        sent.extend(copies)

    def landed(copies):
        for c in copies:
            c.wait_recv()

    left, right = turn(s, z.n_seq - 1, z.n_seq), turn(s, 1, z.n_seq)
    sibling = chip * 2 + (1 - core)
    across = turn(s, z.n_seq - 1 + 2 * core, z.n_seq)

    def chip_peer(k):
        return at(turn(chip, k, z.n_chip) * 2 + core, g)

    def grp_peer(k):
        return at(s, turn(g, k, z.n_grp))

    barrier = pltpu.get_barrier_semaphore()
    peers = [at(sibling, g), at(across, g)]
    peers += [chip_peer(k) for k in range(1, z.n_chip)] + [grp_peer(k) for k in range(1, z.n_grp)]
    for to in peers:
        pl.semaphore_signal(barrier, inc=1, device_id=to, device_id_type=pl.DeviceIdType.MESH)

    for q in range(TAPS * z.gpt):
        j, r = q // z.gpt, (q % z.gpt) * 16
        h = min(16, z.cs - r)
        piece, o = q // z.gpp, (q % z.gpp) * 16
        m["wbuf"][0, piece // 2, piece % 2, o : o + h, :] = conv_ref[j, r : r + h, :]
    for q in range(z.gpt):
        r = q * 16
        h = min(16, z.cs - r)
        piece, o = q // z.ppp, (q % z.ppp) * 16
        m["pbuf"][0, piece // 2, piece % 2, o : o + h, :] = proj_ref[r : r + h, :]
    m["seg"][EDGE : EDGE + z.rows, :] = jnp.broadcast_to(seg_ref[...], (128, z.rows)).T

    pl.semaphore_wait(barrier, len(peers))

    def gather_c(i, buf):
        return [
            remote(buf.at[0, chip, core], buf.at[k, chip, core], m["gc_s"].at[i, k], m["gc_r"].at[i, k], grp_peer(k))
            for k in range(1, z.n_grp)
        ]

    def gather_b(i, buf):
        part = buf.at[pl.ds(1, z.n_grp - 1), chip, core]
        return [
            remote(part, part, m["gb_s"].at[i, k], m["gb_r"].at[i, k], chip_peer(k)) for k in range(1, z.n_chip)
        ]

    def gather_a(i, buf):
        part = buf.at[pl.ds(1, z.n_grp - 1), :, core]
        return [remote(part, part, m["ga_s"].at[i], m["ga_r"].at[i], at(sibling, g))]

    go(pc := gather_c(0, m["pbuf"]))
    halos = []
    ends = (pl.ds(0, EDGE), pl.ds(z.rows - EDGE, EDGE))
    cot_ends = (pl.ds(0, EDGE), pl.ds(z.half - EDGE, EDGE))
    seg_ends = (pl.ds(EDGE, EDGE), pl.ds(z.rows, EDGE))
    for i, (src, dst, cuts) in enumerate(
        ((x_ref, m["xh"], ends), (cot_ref, m["ch"], cot_ends), (m["seg"], m["sh"], seg_ends))
    ):
        for side, to in ((1, left), (0, right)):
            halos.append(remote(
                src.at[cuts[1 - side]], dst.at[side], m["halo_s"].at[2 * i + side], m["halo_r"].at[2 * i + side], at(to, g)
            ))
    go(halos)
    go(wc := gather_c(1, m["wbuf"]))

    def act_rows(first, count):
        def step(t, _):
            b = pl.multiple_of(t * 32, 32)
            r, _inv = normalised(x_ref[pl.ds(b, 32), :].astype(F32))
            cdf = gate(r)
            m["act"][pl.ds(EDGE + b, 32), :] = (r * cdf).astype(BF16).astype(F32)
            m["slope"][pl.ds(b, 32), :] = cdf + r * (jnp.exp(-0.5 * r * r) * (1.0 / math.sqrt(2.0 * math.pi)))
            return 0

        lax.fori_loop(first // 32, (first + count) // 32, step, 0)

    act_rows(0, z.rows // 2)
    landed(pc)
    go(pb := gather_b(0, m["pbuf"]))
    act_rows(z.rows // 2, z.rows // 2)
    landed(wc)
    go(wb := gather_b(1, m["wbuf"]))

    landed(halos)
    for side, where in ((0, 0), (1, EDGE + z.rows)):
        r, _inv = normalised(m["xh"][side].astype(F32))
        m["act"][where : where + EDGE, :] = (r * gate(r)).astype(BF16).astype(F32)
        outside = (s == 0) if side == 0 else (s == z.n_seq - 1)
        m["seg"][where : where + EDGE, :] = jnp.where(outside, -1, m["sh"][side])

    landed(pb)
    go(pa := gather_a(0, m["pbuf"]))

    def spread(src):
        def step(t, _):
            b = pl.multiple_of(t * 64, 64)
            seg = m["seg"][pl.ds(b, 64 + 2 * EDGE), :]
            own = seg[EDGE : EDGE + 64]
            masks = [seg[14 + j : 78 + j] == own for j in range(TAPS)]
            for o in range(0, z.c0, 128):
                window = src[pl.ds(b, 64 + 2 * EDGE), o : o + 128]
                for j in range(TAPS):
                    cut = jnp.where(masks[j], window[14 + j : 78 + j], 0.0).astype(BF16)
                    m["shifted"][pl.ds(b, 64), j * z.c0 + o : j * z.c0 + o + 128] = cut
            return 0

        lax.fori_loop(0, z.rows // 64, step, 0)

    spread(m["act"])

    landed(pa)
    for k in range(z.n_grp):
        base = lax.rem(g + z.n_grp - k, z.n_grp) * z.cs
        for q in range(z.gpt):
            r = q * 16
            h = min(16, z.cs - r)
            piece, o = q // z.ppp, (q % z.ppp) * 16
            rows = m["pbuf"][k, piece // 2, piece % 2, o : o + h, :].astype(z.stage)
            m["pf"][pl.ds(pl.multiple_of(base + r, math.gcd(z.cs, 16)), h), :] = rows
    proj = m["pf"][...].astype(BF16)

    pool_grad = (dot(cot_ref[...], proj, NT) * 0.5).astype(BF16)
    double = pick(256, 128, 0, 2).astype(BF16)
    for t in range(z.half // 128):
        hg = dot(double, pool_grad[t * 128 : t * 128 + 128])
        m["grad"][EDGE + t * 256 : EDGE + t * 256 + 256, :] = hg
        m["gradt"][:, t * 256 : t * 256 + 256] = hg.T.astype(BF16)
    for side, where in ((0, 0), (1, EDGE + z.rows)):
        pg = (dot(m["ch"][side], proj, NT) * 0.5).astype(BF16)
        chosen = pick(EDGE, EDGE, EDGE // 2 if side == 0 else 0, 2).astype(BF16)
        m["grad"][where : where + EDGE, :] = dot(chosen, pg)

    landed(wb)
    go(wa := gather_a(1, m["wbuf"]))

    def unit(u):
        return ("c", u, z.dc) if u < TAPS else ("p", 0, z.dp)

    live = {}

    def reduce_a(u, term):
        n, i, d = unit(u)
        acc = m[n + "_acc"]
        for b in range(z.n_seq):
            acc[i, b // 2, b % 2, 0:d, :] = term[b * d : b * d + d]
        for q in range(z.n_chip):
            m[n + "_sa"][i, q] = acc[i, q, 1 - core].astype(BF16)
        go(c := [remote(m[n + "_sa"].at[i], m[n + "_ra"].at[i], m["ra_s"].at[u], m["ra_r"].at[u], at(sibling, g))])
        live["a", u] = c

    def reduce_b(u):
        n, i, d = unit(u)
        landed(live["a", u])
        for q in range(z.n_chip):
            m[n + "_kb"][i, q] = m[n + "_acc"][i, q, core] + m[n + "_ra"][i, q].astype(F32)
        copies = []
        for k in range(1, z.n_chip):
            m[n + "_sb"][i, k] = m[n + "_kb"][i, turn(chip, k, z.n_chip)].astype(BF16)
            copies.append(remote(
                m[n + "_sb"].at[i, k], m[n + "_rb"].at[i, k], m["rb_s"].at[u, k], m["rb_r"].at[u, k], chip_peer(k)
            ))
        go(copies)
        live["b", u] = copies

    def reduce_c(u):
        n, i, d = unit(u)
        landed(live["b", u])
        total = m[n + "_kb"][i, chip]
        for k in range(1, z.n_chip):
            total = total + m[n + "_rb"][i, k].astype(F32)
        lanes = z.c0 // z.n_grp
        for k in range(z.n_grp):
            m[n + "_kc"][i, k] = total[:, k * lanes : k * lanes + lanes]
        copies = []
        for k in range(1, z.n_grp):
            m[n + "_sc"][i, k] = m[n + "_kc"][i, turn(g, k, z.n_grp)].astype(BF16)
            copies.append(remote(
                m[n + "_sc"].at[i, k], m[n + "_rc"].at[i, k], m["rc_s"].at[u, k], m["rc_r"].at[u, k], grp_peer(k)
            ))
        go(copies)
        live["c", u] = copies

    def reduce_end(u):
        n, i, d = unit(u)
        landed(live["c", u])
        total = m[n + "_kc"][i, g]
        for k in range(1, z.n_grp):
            total = total + m[n + "_rc"][i, k].astype(F32)
        if u < TAPS:
            cg_ref[u] = total[0:d]
        else:
            pg_ref[...] = total[0:d]

    for j in range(TAPS):
        reduce_a(j, dot(m["gradt"][...], m["shifted"][:, j * z.c0 : j * z.c0 + z.c0]))
        if j >= 1:
            reduce_b(j - 1)
        if j >= 3:
            reduce_c(j - 3)

    landed(wa)
    for k in range(z.n_grp):
        base = lax.rem(g + z.n_grp - k, z.n_grp) * z.cs
        for q in range(TAPS * z.gpt):
            j, r = q // z.gpt, (q % z.gpt) * 16
            h = min(16, z.cs - r)
            piece, o = q // z.gpp, (q % z.gpp) * 16
            rows = m["wbuf"][k, piece // 2, piece % 2, o : o + h, :].astype(z.stage)
            place = pl.multiple_of(base + r, math.gcd(z.cs, 16))
            m["wf"][pl.ds(j * z.c0 + place, h), :] = rows
            m["wb"][pl.ds(place, h), (TAPS - 1 - j) * z.c0 : (TAPS - j) * z.c0] = rows
    reduce_b(TAPS - 1)
    reduce_c(2)

    halve = (pick(256, 128, 0, 2).T * 0.5).astype(BF16)
    for t in range(z.rows // 256):
        a = t * 256
        conv = dot(m["shifted"][a : a + 256, :], m["wf"][...].astype(BF16))
        hidden = (x_ref[a : a + 256, :].astype(F32) + conv).astype(BF16)
        m["pooled"][a // 2 : a // 2 + 128, :] = dot(halve, hidden).astype(BF16)
    reduce_c(3)
    pooled = m["pooled"][...]
    reduce_a(TAPS, dot(cot_ref[...].T, pooled))
    po_ref[...] = dot(pooled, proj).astype(BF16)
    reduce_c(4)

    spread(m["grad"])
    reduce_b(TAPS)
    for t in range(z.rows // 256):
        a = t * 256
        act_grad = dot(m["shifted"][a : a + 256, :], m["wb"][...].astype(BF16), NT)
        m["act"][a : a + 256, :] = act_grad * m["slope"][a : a + 256, :]
        if t == 1:
            reduce_c(TAPS)

    def last(t, _):
        b = pl.multiple_of(t * 32, 32)
        r, inverse = normalised(x_ref[pl.ds(b, 32), :].astype(F32))
        ng = m["act"][pl.ds(b, 32), :]
        centred = ng - r * jnp.mean(ng * r, axis=-1, keepdims=True)
        ig_ref[pl.ds(b, 32), :] = (m["grad"][pl.ds(EDGE + b, 32), :] + centred * inverse).astype(BF16)
        return 0

    lax.fori_loop(0, z.rows // 32, last, 0)
    for u in range(TAPS + 1):
        reduce_end(u)
    for c in sent:
        c.wait_send()


def body(mesh, inputs, segment, conv_weight, proj_weight, cotangent):
    z = Sizes(mesh, inputs.shape[1:], conv_weight.shape, proj_weight.shape, cotangent.shape[1:])
    shapes = scratch(z)
    vmem = pl.BlockSpec(memory_space=pltpu.VMEM)
    lanes = z.c0 // z.n_grp
    po, ig, cg, pg = pl.pallas_call(
        functools.partial(kernel, z, tuple(shapes)),
        out_shape=(
            jax.ShapeDtypeStruct((z.half, z.c1), BF16),
            jax.ShapeDtypeStruct((z.rows, z.c0), BF16),
            jax.ShapeDtypeStruct((TAPS, z.dc, lanes), F32),
            jax.ShapeDtypeStruct((z.dp, lanes), F32),
        ),
        in_specs=[vmem] * 5,
        out_specs=[vmem] * 4,
        scratch_shapes=list(shapes.values()),
        compiler_params=pltpu.CompilerParams(
            collective_id=0, has_side_effects=True, vmem_limit_bytes=56 * 1024 * 1024
        ),
    )(inputs[0], segment, conv_weight, proj_weight, cotangent[0])
    return po[None], ig[None], jnp.swapaxes(cg, 1, 2), pg.T


def solution(mesh):
    return jax.shard_map(
        functools.partial(body, mesh),
        mesh=mesh,
        in_specs=(
            P("grp", "seq", None),
            P("grp", "seq"),
            P(None, "grp", None),
            P("grp", None),
            P("grp", "seq", None),
        ),
        out_specs=(
            P("grp", "seq", None),
            P("grp", "seq", None),
            P(None, "grp", "seq"),
            P("grp", "seq"),
        ),
        check_vma=False,
    )
```

```python
import functools
import math

import jax
import jax.numpy as jnp
from jax import lax
from jax.experimental import pallas as pl
from jax.experimental.pallas import tpu as pltpu
from jax.sharding import PartitionSpec as P

F32 = jnp.float32
BF16 = jnp.bfloat16
TAPS = 5
EDGE = 16
NT = (((1,), (1,)), ((), ()))


def up16(n):
    return -(-n // 16) * 16


def dot(a, b, dims=(((1,), (0,)), ((), ()))):
    return lax.dot_general(a, b, dims, preferred_element_type=F32)


def normalised(x):
    inverse = lax.rsqrt(jnp.mean(x * x, axis=-1, keepdims=True) + 1e-06)
    return x * inverse, inverse


def gate(r):
    return 0.5 * (1.0 + lax.erf(r * (1.0 / math.sqrt(2.0))))


def pick(rows, cols, first, per):
    r = lax.broadcasted_iota(jnp.int32, (rows, cols), 0)
    c = lax.broadcasted_iota(jnp.int32, (rows, cols), 1)
    return jnp.where(r // per + first == c, 1.0, 0.0)


class Sizes:
    def __init__(self, mesh, x, conv, proj, cot):
        self.n_seq, self.n_grp = mesh.shape["seq"], mesh.shape["grp"]
        self.n_chip = self.n_seq // 2
        self.rows, self.c0 = x
        self.c1, self.half = cot
        self.cs = conv[1]
        self.gpt = -(-self.cs // 16)
        self.gpp = -(-TAPS * self.gpt // self.n_seq)
        self.ppp = -(-self.gpt // self.n_seq)
        self.parts = 2 if self.gpp % 2 == 0 else 1
        self.gpp //= self.parts
        self.dc, self.dp = self.c0 // self.n_seq, self.c1 // self.n_seq
        self.rc, self.rp = up16(self.dc), up16(self.dp)
        self.stage = BF16 if self.cs % 16 == 0 else F32


def scratch(z):
    ext = z.rows + 2 * EDGE
    V, S = pltpu.VMEM, pltpu.SemaphoreType.DMA
    shapes = dict(
        xh=V((2, EDGE, z.c0), BF16),
        sh=V((2, EDGE, 128), jnp.int32),
        seg=V((ext, 128), jnp.int32),
        act=V((ext, z.c0), F32),
        slope=V((z.rows, z.c0), F32),
        grad=V((ext, z.c0), F32),
        gradt=V((z.c0, z.rows), BF16),
        shifted=V((z.rows, TAPS * z.c0), BF16),
        pooled=V((z.half, z.c0), BF16),
        wbuf=V((z.parts, z.n_grp, z.n_chip, 2, 16 * z.gpp, z.c0), BF16),
        pbuf=V((z.n_grp, z.n_chip, 2, 16 * z.ppp, z.c1), BF16),
        wf=V((TAPS * z.c0, z.c0), z.stage),
        wb=V((z.c0, TAPS * z.c0), z.stage),
        pf=V((z.c0, z.c1), z.stage),
        halo_s=S((6,)),
        halo_r=S((6,)),
        gc_s=S((1 + z.parts, z.n_grp)),
        gc_r=S((1 + z.parts, z.n_grp)),
        gb_s=S((1 + z.parts, z.n_chip)),
        gb_r=S((1 + z.parts, z.n_chip)),
        ga_s=S((1 + z.parts,)),
        ga_r=S((1 + z.parts,)),
        ra_s=S((TAPS + 1,)),
        ra_r=S((TAPS + 1,)),
        rb_s=S((TAPS + 1, z.n_chip)),
        rb_r=S((TAPS + 1, z.n_chip)),
        rc_s=S((TAPS + 1, z.n_grp)),
        rc_r=S((TAPS + 1, z.n_grp)),
    )
    for name, units, r in (("c", TAPS, z.rc), ("p", 1, z.rp)):
        lanes = z.c0 // z.n_grp
        shapes.update({
            name + "_acc": V((units, z.n_chip, 2, r, z.c0), F32),
            name + "_sa": V((units, z.n_chip, r, z.c0), BF16),
            name + "_ra": V((units, z.n_chip, r, z.c0), BF16),
            name + "_kb": V((units, z.n_chip, r, z.c0), F32),
            name + "_sb": V((units, z.n_chip, r, z.c0), BF16),
            name + "_rb": V((units, z.n_chip, r, z.c0), BF16),
            name + "_kc": V((units, z.n_grp, r, lanes), F32),
            name + "_sc": V((units, z.n_grp, r, lanes), BF16),
            name + "_rc": V((units, z.n_grp, r, lanes), BF16),
        })
    return shapes


def kernel(z, names, x_ref, seg_ref, conv_ref, proj_ref, cot_ref, po_ref, ig_ref, cg_ref, pg_ref, *refs):
    m = dict(zip(names, refs))
    s, g = lax.axis_index("seq"), lax.axis_index("grp")
    chip, core = s // 2, s % 2
    sent = []

    def at(s2, g2):
        return {"seq": s2, "grp": g2}

    def turn(i, k, n):
        return lax.rem(i + k, n)

    def remote(src, dst, ss, rs, to):
        return pltpu.make_async_remote_copy(
            src_ref=src, dst_ref=dst, send_sem=ss, recv_sem=rs, device_id=to, device_id_type=pl.DeviceIdType.MESH
        )

    def go(copies):
        for c in copies:
            c.start()
        sent.extend(copies)

    def landed(copies):
        for c in copies:
            c.wait_recv()

    left, right = turn(s, z.n_seq - 1, z.n_seq), turn(s, 1, z.n_seq)
    sibling = chip * 2 + (1 - core)
    across = turn(s, z.n_seq - 1 + 2 * core, z.n_seq)

    def chip_peer(k):
        return at(turn(chip, k, z.n_chip) * 2 + core, g)

    def grp_peer(k):
        return at(s, turn(g, k, z.n_grp))

    barrier = pltpu.get_barrier_semaphore()
    peers = [at(sibling, g), at(across, g)]
    peers += [chip_peer(k) for k in range(1, z.n_chip)] + [grp_peer(k) for k in range(1, z.n_grp)]
    for to in peers:
        pl.semaphore_signal(barrier, inc=1, device_id=to, device_id_type=pl.DeviceIdType.MESH)

    def tap_place(q):
        part, q = divmod(q, z.gpp * z.n_seq)
        return part, q // z.gpp, (q % z.gpp) * 16

    for q in range(TAPS * z.gpt):
        j, r = q // z.gpt, (q % z.gpt) * 16
        h = min(16, z.cs - r)
        part, piece, o = tap_place(q)
        m["wbuf"][part, 0, piece // 2, piece % 2, o : o + h, :] = conv_ref[j, r : r + h, :]
    for q in range(z.gpt):
        r = q * 16
        h = min(16, z.cs - r)
        piece, o = q // z.ppp, (q % z.ppp) * 16
        m["pbuf"][0, piece // 2, piece % 2, o : o + h, :] = proj_ref[r : r + h, :]
    m["seg"][EDGE : EDGE + z.rows, :] = jnp.broadcast_to(seg_ref[...], (128, z.rows)).T

    pl.semaphore_wait(barrier, len(peers))

    def gather_c(i, buf):
        return [
            remote(buf.at[0, chip, core], buf.at[k, chip, core], m["gc_s"].at[i, k], m["gc_r"].at[i, k], grp_peer(k))
            for k in range(1, z.n_grp)
        ]

    def gather_b(i, buf):
        part = buf.at[pl.ds(1, z.n_grp - 1), chip, core]
        return [
            remote(part, part, m["gb_s"].at[i, k], m["gb_r"].at[i, k], chip_peer(k)) for k in range(1, z.n_chip)
        ]

    def gather_a(i, buf):
        part = buf.at[pl.ds(1, z.n_grp - 1), :, core]
        return [remote(part, part, m["ga_s"].at[i], m["ga_r"].at[i], at(sibling, g))]

    go(pc := gather_c(0, m["pbuf"]))
    halos = []
    ends = (pl.ds(0, EDGE), pl.ds(z.rows - EDGE, EDGE))
    seg_ends = (pl.ds(EDGE, EDGE), pl.ds(z.rows, EDGE))
    for i, (src, dst, cuts) in enumerate(
        ((x_ref, m["xh"], ends), (m["seg"], m["sh"], seg_ends))
    ):
        for side, to in ((1, left), (0, right)):
            halos.append(remote(
                src.at[cuts[1 - side]], dst.at[side], m["halo_s"].at[2 * i + side], m["halo_r"].at[2 * i + side], at(to, g)
            ))
    go(halos)
    taps_buf = [m["wbuf"].at[i] for i in range(z.parts)]
    wc = [gather_c(1 + i, buf) for i, buf in enumerate(taps_buf)]
    wb, wa = [None] * z.parts, [None] * z.parts
    for copies in wc:
        go(copies)

    def act_rows(first, count):
        def step(t, _):
            b = pl.multiple_of(t * 32, 32)
            r, _inv = normalised(x_ref[pl.ds(b, 32), :].astype(F32))
            cdf = gate(r)
            m["act"][pl.ds(EDGE + b, 32), :] = (r * cdf).astype(BF16).astype(F32)
            m["slope"][pl.ds(b, 32), :] = cdf + r * (jnp.exp(-0.5 * r * r) * (1.0 / math.sqrt(2.0 * math.pi)))
            return 0

        lax.fori_loop(first // 32, (first + count) // 32, step, 0, unroll=4)

    quarter = z.rows // 4
    act_rows(0, quarter)
    landed(pc)
    go(pb := gather_b(0, m["pbuf"]))
    act_rows(quarter, quarter)
    act_rows(2 * quarter, quarter)
    landed(pb)
    go(pa := gather_a(0, m["pbuf"]))
    landed(wc[0])
    go_b = gather_b(1, taps_buf[0])
    go(go_b)
    wb[0] = go_b
    act_rows(3 * quarter, quarter)

    landed(halos)
    for side, where in ((0, 0), (1, EDGE + z.rows)):
        r, _inv = normalised(m["xh"][side].astype(F32))
        m["act"][where : where + EDGE, :] = (r * gate(r)).astype(BF16).astype(F32)
        outside = (s == 0) if side == 0 else (s == z.n_seq - 1)
        m["seg"][where : where + EDGE, :] = jnp.where(outside, -1, m["sh"][side])

    def spread(src):
        def step(t, _):
            b = pl.multiple_of(t * 64, 64)
            seg = m["seg"][pl.ds(b, 64 + 2 * EDGE), :]
            own = seg[EDGE : EDGE + 64]
            masks = [seg[14 + j : 78 + j] == own for j in range(TAPS)]
            for o in range(0, z.c0, 128):
                window = src[pl.ds(b, 64 + 2 * EDGE), o : o + 128]
                for j in range(TAPS):
                    cut = jnp.where(masks[j], window[14 + j : 78 + j], 0.0).astype(BF16)
                    m["shifted"][pl.ds(b, 64), j * z.c0 + o : j * z.c0 + o + 128] = cut
            return 0

        lax.fori_loop(0, z.rows // 64, step, 0, unroll=2)

    for i in range(1, z.parts):
        landed(wc[i])
        wb[i] = gather_b(1 + i, taps_buf[i])
        go(wb[i])
    spread(m["act"])

    landed(pa)
    for k in range(z.n_grp):
        base = lax.rem(g + z.n_grp - k, z.n_grp) * z.cs
        for q in range(z.gpt):
            r = q * 16
            h = min(16, z.cs - r)
            piece, o = q // z.ppp, (q % z.ppp) * 16
            rows = m["pbuf"][k, piece // 2, piece % 2, o : o + h, :].astype(z.stage)
            m["pf"][pl.ds(pl.multiple_of(base + r, math.gcd(z.cs, 16)), h), :] = rows
    proj = m["pf"][...].astype(BF16)

    pool_grad = (dot(proj, cot_ref[...]) * 0.5).astype(BF16)
    double = pick(256, 128, 0, 2)
    double_t = double.T.astype(BF16)
    double = double.astype(BF16)
    for t in range(z.half // 128):
        block = pool_grad[:, t * 128 : t * 128 + 128]
        m["grad"][EDGE + t * 256 : EDGE + t * 256 + 256, :] = dot(double, block, NT)
        m["gradt"][:, t * 256 : t * 256 + 256] = dot(block, double_t).astype(BF16)
    edges = []
    for i, (src, dst, to) in enumerate(((EDGE, EDGE + z.rows, left), (EDGE + z.rows - 8, EDGE - 8, right))):
        edges.append(remote(
            m["grad"].at[pl.ds(src, 8)], m["grad"].at[pl.ds(dst, 8)], m["halo_s"].at[4 + i], m["halo_r"].at[4 + i], at(to, g)
        ))
    go(edges)
    proj_t = proj.T

    landed(wb[0])
    wa[0] = gather_a(1, taps_buf[0])
    go(wa[0])

    def unit(u):
        return ("c", u, z.dc) if u < TAPS else ("p", 0, z.dp)

    live = {}

    def reduce_a(u, term):
        n, i, d = unit(u)
        acc = m[n + "_acc"]
        for b in range(z.n_seq):
            acc[i, b // 2, b % 2, 0:d, :] = term[b * d : b * d + d]
        for q in range(z.n_chip):
            m[n + "_sa"][i, q] = acc[i, q, 1 - core].astype(BF16)
        go(c := [remote(m[n + "_sa"].at[i], m[n + "_ra"].at[i], m["ra_s"].at[u], m["ra_r"].at[u], at(sibling, g))])
        live["a", u] = c

    def reduce_b(u):
        n, i, d = unit(u)
        landed(live["a", u])
        for q in range(z.n_chip):
            m[n + "_kb"][i, q] = m[n + "_acc"][i, q, core] + m[n + "_ra"][i, q].astype(F32)
        copies = []
        for k in range(1, z.n_chip):
            m[n + "_sb"][i, k] = m[n + "_kb"][i, turn(chip, k, z.n_chip)].astype(BF16)
            copies.append(remote(
                m[n + "_sb"].at[i, k], m[n + "_rb"].at[i, k], m["rb_s"].at[u, k], m["rb_r"].at[u, k], chip_peer(k)
            ))
        go(copies)
        live["b", u] = copies

    def reduce_c(u):
        n, i, d = unit(u)
        landed(live["b", u])
        total = m[n + "_kb"][i, chip]
        for k in range(1, z.n_chip):
            total = total + m[n + "_rb"][i, k].astype(F32)
        lanes = z.c0 // z.n_grp
        for k in range(z.n_grp):
            m[n + "_kc"][i, k] = total[:, k * lanes : k * lanes + lanes]
        copies = []
        for k in range(1, z.n_grp):
            m[n + "_sc"][i, k] = m[n + "_kc"][i, turn(g, k, z.n_grp)].astype(BF16)
            copies.append(remote(
                m[n + "_sc"].at[i, k], m[n + "_rc"].at[i, k], m["rc_s"].at[u, k], m["rc_r"].at[u, k], grp_peer(k)
            ))
        go(copies)
        live["c", u] = copies

    def reduce_end(u):
        n, i, d = unit(u)
        landed(live["c", u])
        total = m[n + "_kc"][i, g]
        for k in range(1, z.n_grp):
            total = total + m[n + "_rc"][i, k].astype(F32)
        if u < TAPS:
            cg_ref[u] = total[0:d]
        else:
            pg_ref[...] = total[0:d]

    for j in range(TAPS):
        reduce_a(j, dot(m["gradt"][...], m["shifted"][:, j * z.c0 : j * z.c0 + z.c0]))
        if j >= 2:
            reduce_b(j - 2)
        if j == 2:
            for i in range(1, z.parts):
                landed(wb[i])
                wa[i] = gather_a(1 + i, taps_buf[i])
                go(wa[i])

    for copies in wa:
        landed(copies)
    for k in range(z.n_grp):
        base = lax.rem(g + z.n_grp - k, z.n_grp) * z.cs
        for q in range(TAPS * z.gpt):
            j, r = q // z.gpt, (q % z.gpt) * 16
            h = min(16, z.cs - r)
            part, piece, o = tap_place(q)
            rows = m["wbuf"][part, k, piece // 2, piece % 2, o : o + h, :].astype(z.stage)
            place = pl.multiple_of(base + r, math.gcd(z.cs, 16))
            m["wf"][pl.ds(j * z.c0 + place, h), :] = rows
            m["wb"][pl.ds(place, h), (TAPS - 1 - j) * z.c0 : (TAPS - j) * z.c0] = rows
    reduce_b(3)
    reduce_b(4)

    halve = (pick(256, 128, 0, 2).T * 0.5).astype(BF16)
    for t in range(z.rows // 256):
        a = t * 256
        conv = dot(m["shifted"][a : a + 256, :], m["wf"][...].astype(BF16))
        hidden = (x_ref[a : a + 256, :].astype(F32) + conv).astype(BF16)
        m["pooled"][a // 2 : a // 2 + 128, :] = dot(halve, hidden).astype(BF16)
    pooled = m["pooled"][...]
    reduce_a(TAPS, dot(cot_ref[...], pooled))
    reduce_c(0)
    reduce_c(1)
    po_ref[...] = dot(proj_t, pooled, NT).astype(BF16)

    landed(edges)
    spread(m["grad"])
    reduce_b(TAPS)
    reduce_c(2)
    for t in range(z.rows // 256):
        a = t * 256
        act_grad = dot(m["shifted"][a : a + 256, :], m["wb"][...].astype(BF16), NT)
        m["act"][a : a + 256, :] = act_grad * m["slope"][a : a + 256, :]
        if t == 1:
            reduce_c(3)
    reduce_c(4)

    def last(t, _):
        b = pl.multiple_of(t * 32, 32)
        r, inverse = normalised(x_ref[pl.ds(b, 32), :].astype(F32))
        ng = m["act"][pl.ds(b, 32), :]
        centred = ng - r * jnp.mean(ng * r, axis=-1, keepdims=True)
        ig_ref[pl.ds(b, 32), :] = (m["grad"][pl.ds(EDGE + b, 32), :] + centred * inverse).astype(BF16)
        return 0

    lax.fori_loop(0, z.rows // 64, last, 0, unroll=4)
    reduce_c(TAPS)
    lax.fori_loop(z.rows // 64, z.rows // 32, last, 0, unroll=4)
    for u in range(TAPS + 1):
        reduce_end(u)
    for c in sent:
        c.wait_send()


def body(mesh, inputs, segment, conv_weight, proj_weight, cotangent):
    z = Sizes(mesh, inputs.shape[1:], conv_weight.shape, proj_weight.shape, cotangent.shape[:0:-1])
    shapes = scratch(z)
    vmem = pl.BlockSpec(memory_space=pltpu.VMEM)
    lanes = z.c0 // z.n_grp
    po, ig, cg, pg = pl.pallas_call(
        functools.partial(kernel, z, tuple(shapes)),
        out_shape=(
            jax.ShapeDtypeStruct((z.c1, z.half), BF16),
            jax.ShapeDtypeStruct((z.rows, z.c0), BF16),
            jax.ShapeDtypeStruct((TAPS, z.dc, lanes), F32),
            jax.ShapeDtypeStruct((z.dp, lanes), F32),
        ),
        in_specs=[vmem] * 5,
        out_specs=[vmem] * 4,
        scratch_shapes=list(shapes.values()),
        compiler_params=pltpu.CompilerParams(
            collective_id=0, has_side_effects=True, vmem_limit_bytes=56 * 1024 * 1024
        ),
    )(inputs[0], segment, conv_weight, proj_weight, cotangent[0].T)
    return po.T[None], ig[None], jnp.swapaxes(cg, 1, 2), pg.T


def solution(mesh):
    return jax.shard_map(
        functools.partial(body, mesh),
        mesh=mesh,
        in_specs=(
            P("grp", "seq", None),
            P("grp", "seq"),
            P(None, "grp", None),
            P("grp", None),
            P("grp", "seq", None),
        ),
        out_specs=(
            P("grp", "seq", None),
            P("grp", "seq", None),
            P(None, "grp", "seq"),
            P("grp", "seq"),
        ),
        check_vma=False,
    )
```

```python
import functools
import math

import jax
import jax.numpy as jnp
from jax import lax
from jax.experimental import pallas as pl
from jax.experimental.pallas import tpu as pltpu
from jax.sharding import PartitionSpec as P

F32 = jnp.float32
BF16 = jnp.bfloat16
TAPS = 5
EDGE = 16
NT = (((1,), (1,)), ((), ()))


def up16(n):
    return -(-n // 16) * 16


def dot(a, b, dims=(((1,), (0,)), ((), ()))):
    return lax.dot_general(a, b, dims, preferred_element_type=F32)


def normalised(x):
    inverse = lax.rsqrt(jnp.mean(x * x, axis=-1, keepdims=True) + 1e-06)
    return x * inverse, inverse


def gate(r):
    return 0.5 * (1.0 + lax.erf(r * (1.0 / math.sqrt(2.0))))


def pick(rows, cols, first, per):
    r = lax.broadcasted_iota(jnp.int32, (rows, cols), 0)
    c = lax.broadcasted_iota(jnp.int32, (rows, cols), 1)
    return jnp.where(r // per + first == c, 1.0, 0.0)


class Sizes:
    def __init__(self, mesh, x, conv, proj, cot):
        self.n_seq, self.n_grp = mesh.shape["seq"], mesh.shape["grp"]
        self.n_chip = self.n_seq // 2
        self.rows, self.c0 = x
        self.c1, self.half = cot
        self.cs = conv[1]
        self.gpt = -(-self.cs // 16)
        self.gpp = -(-TAPS * self.gpt // self.n_seq)
        self.ppp = -(-self.gpt // self.n_seq)
        self.parts = self.gpp if self.gpp <= 4 else 1
        self.gpp //= self.parts
        self.dc, self.dp = self.c0 // self.n_seq, self.c1 // self.n_seq
        self.rc, self.rp = up16(self.dc), up16(self.dp)
        self.stage = BF16 if self.cs % 16 == 0 else F32


def scratch(z):
    ext = z.rows + 2 * EDGE
    V, S = pltpu.VMEM, pltpu.SemaphoreType.DMA
    shapes = dict(
        xh=V((2, EDGE, z.c0), BF16),
        sh=V((2, EDGE, 128), jnp.int32),
        seg=V((ext, 128), jnp.int32),
        act=V((ext, z.c0), F32),
        slope=V((z.rows, z.c0), F32),
        grad=V((ext, z.c0), F32),
        gradt=V((z.c0, z.rows), BF16),
        shifted=V((z.rows, TAPS * z.c0), BF16),
        pooled=V((z.half, z.c0), BF16),
        wbuf=V((z.parts, z.n_grp, z.n_chip, 2, 16 * z.gpp, z.c0), BF16),
        pbuf=V((z.n_grp, z.n_chip, 2, 16 * z.ppp, z.c1), BF16),
        wf=V((TAPS * z.c0, z.c0), z.stage),
        wb=V((z.c0, TAPS * z.c0), z.stage),
        pf=V((z.c0, z.c1), z.stage),
        halo_s=S((6,)),
        halo_r=S((6,)),
        gc_s=S((1 + z.parts, z.n_grp)),
        gc_r=S((1 + z.parts, z.n_grp)),
        gb_s=S((1 + z.parts, z.n_chip)),
        gb_r=S((1 + z.parts, z.n_chip)),
        ga_s=S((1 + z.parts,)),
        ga_r=S((1 + z.parts,)),
        ra_s=S((TAPS + 1,)),
        ra_r=S((TAPS + 1,)),
        rb_s=S((TAPS + 1, z.n_chip)),
        rb_r=S((TAPS + 1, z.n_chip)),
        rc_s=S((TAPS + 1, z.n_grp)),
        rc_r=S((TAPS + 1, z.n_grp)),
    )
    for name, units, r in (("c", TAPS, z.rc), ("p", 1, z.rp)):
        lanes = z.c0 // z.n_grp
        shapes.update({
            name + "_acc": V((units, z.n_chip, 2, r, z.c0), F32),
            name + "_sa": V((units, z.n_chip, r, z.c0), BF16),
            name + "_ra": V((units, z.n_chip, r, z.c0), BF16),
            name + "_kb": V((units, z.n_chip, r, z.c0), F32),
            name + "_sb": V((units, z.n_chip, r, z.c0), BF16),
            name + "_rb": V((units, z.n_chip, r, z.c0), BF16),
            name + "_kc": V((units, z.n_grp, r, lanes), F32),
            name + "_sc": V((units, z.n_grp, r, lanes), BF16),
            name + "_rc": V((units, z.n_grp, r, lanes), BF16),
        })
    return shapes


def kernel(z, names, x_ref, seg_ref, conv_ref, proj_ref, cot_ref, po_ref, ig_ref, cg_ref, pg_ref, *refs):
    m = dict(zip(names, refs))
    s, g = lax.axis_index("seq"), lax.axis_index("grp")
    chip, core = s // 2, s % 2
    sent = []

    def at(s2, g2):
        return {"seq": s2, "grp": g2}

    def turn(i, k, n):
        return lax.rem(i + k, n)

    def remote(src, dst, ss, rs, to):
        return pltpu.make_async_remote_copy(
            src_ref=src, dst_ref=dst, send_sem=ss, recv_sem=rs, device_id=to, device_id_type=pl.DeviceIdType.MESH
        )

    def go(copies):
        for c in copies:
            c.start()
        sent.extend(copies)

    def landed(copies):
        for c in copies:
            c.wait_recv()

    left, right = turn(s, z.n_seq - 1, z.n_seq), turn(s, 1, z.n_seq)
    sibling = chip * 2 + (1 - core)
    across = turn(s, z.n_seq - 1 + 2 * core, z.n_seq)

    def chip_peer(k):
        return at(turn(chip, k, z.n_chip) * 2 + core, g)

    def grp_peer(k):
        return at(s, turn(g, k, z.n_grp))

    barrier = pltpu.get_barrier_semaphore()
    peers = [at(sibling, g), at(across, g)]
    peers += [chip_peer(k) for k in range(1, z.n_chip)] + [grp_peer(k) for k in range(1, z.n_grp)]
    for to in peers:
        pl.semaphore_signal(barrier, inc=1, device_id=to, device_id_type=pl.DeviceIdType.MESH)

    def tap_place(q):
        part, q = divmod(q, z.gpp * z.n_seq)
        return part, q // z.gpp, (q % z.gpp) * 16

    for q in range(TAPS * z.gpt):
        j, r = q // z.gpt, (q % z.gpt) * 16
        h = min(16, z.cs - r)
        part, piece, o = tap_place(q)
        m["wbuf"][part, 0, piece // 2, piece % 2, o : o + h, :] = conv_ref[j, r : r + h, :]
    for q in range(z.gpt):
        r = q * 16
        h = min(16, z.cs - r)
        piece, o = q // z.ppp, (q % z.ppp) * 16
        m["pbuf"][0, piece // 2, piece % 2, o : o + h, :] = proj_ref[r : r + h, :]
    m["seg"][EDGE : EDGE + z.rows, :] = jnp.broadcast_to(seg_ref[...], (128, z.rows)).T

    pl.semaphore_wait(barrier, len(peers))

    def gather_c(i, buf):
        return [
            remote(buf.at[0, chip, core], buf.at[k, chip, core], m["gc_s"].at[i, k], m["gc_r"].at[i, k], grp_peer(k))
            for k in range(1, z.n_grp)
        ]

    def gather_b(i, buf):
        part = buf.at[pl.ds(1, z.n_grp - 1), chip, core]
        return [
            remote(part, part, m["gb_s"].at[i, k], m["gb_r"].at[i, k], chip_peer(k)) for k in range(1, z.n_chip)
        ]

    def gather_a(i, buf):
        part = buf.at[pl.ds(1, z.n_grp - 1), :, core]
        return [remote(part, part, m["ga_s"].at[i], m["ga_r"].at[i], at(sibling, g))]

    go(pc := gather_c(0, m["pbuf"]))
    halos = []
    ends = (pl.ds(0, EDGE), pl.ds(z.rows - EDGE, EDGE))
    seg_ends = (pl.ds(EDGE, EDGE), pl.ds(z.rows, EDGE))
    for i, (src, dst, cuts) in enumerate(
        ((x_ref, m["xh"], ends), (m["seg"], m["sh"], seg_ends))
    ):
        for side, to in ((1, left), (0, right)):
            halos.append(remote(
                src.at[cuts[1 - side]], dst.at[side], m["halo_s"].at[2 * i + side], m["halo_r"].at[2 * i + side], at(to, g)
            ))
    go(halos)
    taps_buf = [m["wbuf"].at[i] for i in range(z.parts)]
    wc = [gather_c(1 + i, buf) for i, buf in enumerate(taps_buf)]
    wb, wa = [None] * z.parts, [None] * z.parts
    for copies in wc:
        go(copies)

    def act_rows(first, count):
        def step(t, _):
            b = pl.multiple_of(t * 32, 32)
            r, _inv = normalised(x_ref[pl.ds(b, 32), :].astype(F32))
            cdf = gate(r)
            m["act"][pl.ds(EDGE + b, 32), :] = (r * cdf).astype(BF16).astype(F32)
            m["slope"][pl.ds(b, 32), :] = cdf + r * (jnp.exp(-0.5 * r * r) * (1.0 / math.sqrt(2.0 * math.pi)))
            return 0

        lax.fori_loop(first // 32, (first + count) // 32, step, 0, unroll=4)

    def forward_b(i):
        if i < z.parts:
            landed(wc[i])
            wb[i] = gather_b(1 + i, taps_buf[i])
            go(wb[i])

    def forward_a(i):
        if i < z.parts:
            landed(wb[i])
            wa[i] = gather_a(1 + i, taps_buf[i])
            go(wa[i])

    half = z.rows // 2
    act_rows(0, half)
    landed(pc)
    go(pb := gather_b(0, m["pbuf"]))
    act_rows(half, half)
    forward_b(0)

    landed(halos)
    for side, where in ((0, 0), (1, EDGE + z.rows)):
        r, _inv = normalised(m["xh"][side].astype(F32))
        m["act"][where : where + EDGE, :] = (r * gate(r)).astype(BF16).astype(F32)
        outside = (s == 0) if side == 0 else (s == z.n_seq - 1)
        m["seg"][where : where + EDGE, :] = jnp.where(outside, -1, m["sh"][side])

    def spread(src, part):
        def step(t, _):
            b = pl.multiple_of(t * 64, 64)
            seg = m["seg"][pl.ds(b, 64 + 2 * EDGE), :]
            own = seg[EDGE : EDGE + 64]
            masks = [seg[14 + j : 78 + j] == own for j in range(TAPS)]
            for o in range(0, z.c0, 128):
                window = src[pl.ds(b, 64 + 2 * EDGE), o : o + 128]
                for j in range(TAPS):
                    cut = jnp.where(masks[j], window[14 + j : 78 + j], 0.0).astype(BF16)
                    m["shifted"][pl.ds(b, 64), j * z.c0 + o : j * z.c0 + o + 128] = cut
            return 0

        n = z.rows // 128
        lax.fori_loop(part * n, part * n + n, step, 0, unroll=2)

    spread(m["act"], 0)
    forward_b(1)
    landed(pb)
    go(pa := gather_a(0, m["pbuf"]))
    spread(m["act"], 1)
    forward_b(2)

    landed(pa)
    for k in range(z.n_grp):
        base = lax.rem(g + z.n_grp - k, z.n_grp) * z.cs
        for q in range(z.gpt):
            r = q * 16
            h = min(16, z.cs - r)
            piece, o = q // z.ppp, (q % z.ppp) * 16
            rows = m["pbuf"][k, piece // 2, piece % 2, o : o + h, :].astype(z.stage)
            m["pf"][pl.ds(pl.multiple_of(base + r, math.gcd(z.cs, 16)), h), :] = rows
    proj = m["pf"][...].astype(BF16)

    pool_grad = (dot(proj, cot_ref[...]) * 0.5).astype(BF16)
    double = pick(256, 128, 0, 2)
    double_t = double.T.astype(BF16)
    double = double.astype(BF16)
    for t in range(z.half // 128):
        block = pool_grad[:, t * 128 : t * 128 + 128]
        m["grad"][EDGE + t * 256 : EDGE + t * 256 + 256, :] = dot(double, block, NT)
        m["gradt"][:, t * 256 : t * 256 + 256] = dot(block, double_t).astype(BF16)
    edges = []
    for i, (src, dst, to) in enumerate(((EDGE, EDGE + z.rows, left), (EDGE + z.rows - 8, EDGE - 8, right))):
        edges.append(remote(
            m["grad"].at[pl.ds(src, 8)], m["grad"].at[pl.ds(dst, 8)], m["halo_s"].at[4 + i], m["halo_r"].at[4 + i], at(to, g)
        ))
    go(edges)
    proj_t = proj.T

    forward_b(3)
    forward_a(0)

    def unit(u):
        return ("c", u, z.dc) if u < TAPS else ("p", 0, z.dp)

    live = {}

    def reduce_a(u, term):
        n, i, d = unit(u)
        acc = m[n + "_acc"]
        for b in range(z.n_seq):
            acc[i, b // 2, b % 2, 0:d, :] = term[b * d : b * d + d]
        for q in range(z.n_chip):
            m[n + "_sa"][i, q] = acc[i, q, 1 - core].astype(BF16)
        go(c := [remote(m[n + "_sa"].at[i], m[n + "_ra"].at[i], m["ra_s"].at[u], m["ra_r"].at[u], at(sibling, g))])
        live["a", u] = c

    def reduce_b(u):
        n, i, d = unit(u)
        landed(live["a", u])
        for q in range(z.n_chip):
            m[n + "_kb"][i, q] = m[n + "_acc"][i, q, core] + m[n + "_ra"][i, q].astype(F32)
        copies = []
        for k in range(1, z.n_chip):
            m[n + "_sb"][i, k] = m[n + "_kb"][i, turn(chip, k, z.n_chip)].astype(BF16)
            copies.append(remote(
                m[n + "_sb"].at[i, k], m[n + "_rb"].at[i, k], m["rb_s"].at[u, k], m["rb_r"].at[u, k], chip_peer(k)
            ))
        go(copies)
        live["b", u] = copies

    def reduce_c(u):
        n, i, d = unit(u)
        landed(live["b", u])
        total = m[n + "_kb"][i, chip]
        for k in range(1, z.n_chip):
            total = total + m[n + "_rb"][i, k].astype(F32)
        lanes = z.c0 // z.n_grp
        for k in range(z.n_grp):
            m[n + "_kc"][i, k] = total[:, k * lanes : k * lanes + lanes]
        copies = []
        for k in range(1, z.n_grp):
            m[n + "_sc"][i, k] = m[n + "_kc"][i, turn(g, k, z.n_grp)].astype(BF16)
            copies.append(remote(
                m[n + "_sc"].at[i, k], m[n + "_rc"].at[i, k], m["rc_s"].at[u, k], m["rc_r"].at[u, k], grp_peer(k)
            ))
        go(copies)
        live["c", u] = copies

    def reduce_end(u):
        n, i, d = unit(u)
        landed(live["c", u])
        total = m[n + "_kc"][i, g]
        for k in range(1, z.n_grp):
            total = total + m[n + "_rc"][i, k].astype(F32)
        if u < TAPS:
            cg_ref[u] = total[0:d]
        else:
            pg_ref[...] = total[0:d]

    for j in range(TAPS):
        reduce_a(j, dot(m["gradt"][...], m["shifted"][:, j * z.c0 : j * z.c0 + z.c0]))
        if j == 1:
            forward_a(1)
        if j == 3:
            forward_a(2)

    def assemble(i):
        if i >= z.parts:
            return
        landed(wa[i])
        for k in range(z.n_grp):
            base = lax.rem(g + z.n_grp - k, z.n_grp) * z.cs
            for q in range(TAPS * z.gpt):
                part, piece, o = tap_place(q)
                if part != i:
                    continue
                j, r = q // z.gpt, (q % z.gpt) * 16
                h = min(16, z.cs - r)
                rows = m["wbuf"][part, k, piece // 2, piece % 2, o : o + h, :].astype(z.stage)
                place = pl.multiple_of(base + r, math.gcd(z.cs, 16))
                m["wf"][pl.ds(j * z.c0 + place, h), :] = rows
                m["wb"][pl.ds(place, h), (TAPS - 1 - j) * z.c0 : (TAPS - j) * z.c0] = rows

    reduce_b(0)
    assemble(0)
    assemble(1)
    reduce_b(1)
    forward_a(3)
    reduce_b(2)
    assemble(2)
    reduce_b(3)
    reduce_b(4)
    assemble(3)

    halve = (pick(256, 128, 0, 2).T * 0.5).astype(BF16)
    for t in range(z.rows // 256):
        a = t * 256
        conv = dot(m["shifted"][a : a + 256, :], m["wf"][...].astype(BF16))
        hidden = (x_ref[a : a + 256, :].astype(F32) + conv).astype(BF16)
        m["pooled"][a // 2 : a // 2 + 128, :] = dot(halve, hidden).astype(BF16)
    pooled = m["pooled"][...]
    reduce_a(TAPS, dot(cot_ref[...], pooled))
    reduce_c(0)
    reduce_c(1)
    po_ref[...] = dot(proj_t, pooled, NT).astype(BF16)

    landed(edges)
    spread(m["grad"], 0)
    reduce_b(TAPS)
    reduce_c(2)
    spread(m["grad"], 1)

    def last(t, _):
        b = pl.multiple_of(t * 32, 32)
        r, inverse = normalised(x_ref[pl.ds(b, 32), :].astype(F32))
        ng = m["act"][pl.ds(b, 32), :]
        centred = ng - r * jnp.mean(ng * r, axis=-1, keepdims=True)
        ig_ref[pl.ds(b, 32), :] = (m["grad"][pl.ds(EDGE + b, 32), :] + centred * inverse).astype(BF16)
        return 0

    for t in range(z.rows // 256):
        a = t * 256
        act_grad = dot(m["shifted"][a : a + 256, :], m["wb"][...].astype(BF16), NT)
        m["act"][a : a + 256, :] = act_grad * m["slope"][a : a + 256, :]
        if t == 0:
            reduce_c(3)
        if t == 1:
            reduce_c(4)
        if t == 2:
            reduce_c(TAPS)
        lax.fori_loop(a // 32, a // 32 + 8, last, 0, unroll=4)
    for u in range(TAPS + 1):
        reduce_end(u)
    for c in sent:
        c.wait_send()


def finish(*refs):
    ins, outs, held, came, left = refs[:4], refs[4:8], refs[8:12], refs[12], refs[13]
    first = [pltpu.make_async_copy(a, b, came.at[i]) for i, (a, b) in enumerate(zip(ins, held))]
    then = [pltpu.make_async_copy(a, b, left.at[i]) for i, (a, b) in enumerate(zip(held, outs))]
    for c in first:
        c.start()
    for c, d in zip(first, then):
        c.wait()
        d.start()
    for d in then:
        d.wait()


def body(mesh, inputs, segment, conv_weight, proj_weight, cotangent):
    z = Sizes(mesh, inputs.shape[1:], conv_weight.shape, proj_weight.shape, cotangent.shape[:0:-1])
    shapes = scratch(z)
    vmem = pl.BlockSpec(memory_space=pltpu.VMEM)
    lanes = z.c0 // z.n_grp
    po, ig, cg, pg = pl.pallas_call(
        functools.partial(kernel, z, tuple(shapes)),
        out_shape=(
            jax.ShapeDtypeStruct((z.c1, z.half), BF16),
            jax.ShapeDtypeStruct((z.rows, z.c0), BF16),
            jax.ShapeDtypeStruct((TAPS, z.dc, lanes), F32),
            jax.ShapeDtypeStruct((z.dp, lanes), F32),
        ),
        in_specs=[vmem] * 5,
        out_specs=[vmem] * 4,
        scratch_shapes=list(shapes.values()),
        compiler_params=pltpu.CompilerParams(
            collective_id=0, has_side_effects=True, vmem_limit_bytes=56 * 1024 * 1024
        ),
    )(inputs[0], segment, conv_weight, proj_weight, cotangent[0].T)
    outs = (po, ig, cg, pg)
    po, ig, cg, pg = pl.pallas_call(
        finish,
        out_shape=tuple(jax.ShapeDtypeStruct(o.shape, o.dtype) for o in outs),
        in_specs=[pl.BlockSpec(memory_space=pl.ANY)] * 4,
        out_specs=[pl.BlockSpec(memory_space=pl.ANY)] * 4,
        scratch_shapes=[pltpu.VMEM(o.shape, o.dtype) for o in outs] + [pltpu.SemaphoreType.DMA((4,))] * 2,
        compiler_params=pltpu.CompilerParams(vmem_limit_bytes=56 * 1024 * 1024),
    )(*outs)
    return po.T[None], ig[None], jnp.swapaxes(cg, 1, 2), pg.T


def solution(mesh):
    return jax.shard_map(
        functools.partial(body, mesh),
        mesh=mesh,
        in_specs=(
            P("grp", "seq", None),
            P("grp", "seq"),
            P(None, "grp", None),
            P("grp", None),
            P("grp", "seq", None),
        ),
        out_specs=(
            P("grp", "seq", None),
            P("grp", "seq", None),
            P(None, "grp", "seq"),
            P("grp", "seq"),
        ),
        check_vma=False,
    )
```

```python
import functools
import math

import jax
import jax.numpy as jnp
from jax import lax
from jax.experimental import pallas as pl
from jax.experimental.pallas import tpu as pltpu
from jax.sharding import PartitionSpec as P

F32 = jnp.float32
BF16 = jnp.bfloat16
TAPS = 5
EDGE = 16
NT = (((1,), (1,)), ((), ()))


def up16(n):
    return -(-n // 16) * 16


def dot(a, b, dims=(((1,), (0,)), ((), ()))):
    return lax.dot_general(a, b, dims, preferred_element_type=F32)


def normalised(x):
    inverse = lax.rsqrt(jnp.mean(x * x, axis=-1, keepdims=True) + 1e-06)
    return x * inverse, inverse


def gate(r):
    return 0.5 * (1.0 + lax.erf(r * (1.0 / math.sqrt(2.0))))


def pick(rows, cols, first, per):
    r = lax.broadcasted_iota(jnp.int32, (rows, cols), 0)
    c = lax.broadcasted_iota(jnp.int32, (rows, cols), 1)
    return jnp.where(r // per + first == c, 1.0, 0.0)


class Sizes:
    def __init__(self, mesh, x, conv, proj, cot):
        self.n_seq, self.n_grp = mesh.shape["seq"], mesh.shape["grp"]
        self.n_chip = self.n_seq // 2
        self.rows, self.c0 = x
        self.c1, self.half = cot
        self.cs = conv[1]
        self.gpt = -(-self.cs // 16)
        self.gpp = -(-TAPS * self.gpt // self.n_seq)
        self.ppp = -(-self.gpt // self.n_seq)
        self.parts = self.gpp if self.gpp <= 4 else 1
        self.gpp //= self.parts
        self.dc, self.dp = self.c0 // self.n_seq, self.c1 // self.n_seq
        self.rc, self.rp = up16(self.dc), up16(self.dp)
        self.stage = BF16 if self.cs % 16 == 0 else F32


def scratch(z):
    ext = z.rows + 2 * EDGE
    V, S = pltpu.VMEM, pltpu.SemaphoreType.DMA
    shapes = dict(
        xh=V((2, EDGE, z.c0), BF16),
        sh=V((2, EDGE, 128), jnp.int32),
        seg=V((ext, 128), jnp.int32),
        act=V((ext, z.c0), F32),
        slope=V((z.rows, z.c0), F32),
        grad=V((ext, z.c0), F32),
        gradt=V((z.c0, z.rows), BF16),
        shifted=V((z.rows, TAPS * z.c0), BF16),
        pooled=V((z.half, z.c0), BF16),
        wbuf=V((z.parts, z.n_grp, z.n_chip, 2, 16 * z.gpp, z.c0), BF16),
        pbuf=V((z.n_grp, z.n_chip, 2, 16 * z.ppp, z.c1), BF16),
        wf=V((TAPS * z.c0, z.c0), z.stage),
        wb=V((z.c0, TAPS * z.c0), z.stage),
        pf=V((z.c0, z.c1), z.stage),
        halo_s=S((6,)),
        halo_r=S((6,)),
        gc_s=S((1 + z.parts, z.n_grp)),
        gc_r=S((1 + z.parts, z.n_grp)),
        gb_s=S((1 + z.parts, z.n_chip)),
        gb_r=S((1 + z.parts, z.n_chip)),
        ga_s=S((1 + z.parts,)),
        ga_r=S((1 + z.parts,)),
        ra_s=S((TAPS + 1,)),
        ra_r=S((TAPS + 1,)),
        rb_s=S((TAPS + 1, z.n_chip)),
        rb_r=S((TAPS + 1, z.n_chip)),
        rc_s=S((TAPS + 1, z.n_grp)),
        rc_r=S((TAPS + 1, z.n_grp)),
    )
    for name, units, r in (("c", TAPS, z.rc), ("p", 1, z.rp)):
        lanes = z.c0 // z.n_grp
        shapes.update({
            name + "_acc": V((units, z.n_chip, 2, r, z.c0), F32),
            name + "_sa": V((units, z.n_chip, r, z.c0), BF16),
            name + "_ra": V((units, z.n_chip, r, z.c0), BF16),
            name + "_kb": V((units, z.n_chip, r, z.c0), F32),
            name + "_sb": V((units, z.n_chip, r, z.c0), BF16),
            name + "_rb": V((units, z.n_chip, r, z.c0), BF16),
            name + "_kc": V((units, z.n_grp, r, lanes), F32),
            name + "_sc": V((units, z.n_grp, r, lanes), BF16),
            name + "_rc": V((units, z.n_grp, r, lanes), BF16),
        })
    return shapes


def kernel(z, names, x_ref, seg_ref, conv_ref, proj_ref, cot_ref, po_ref, ig_ref, cg_ref, pg_ref, *refs):
    m = dict(zip(names, refs))
    s, g = lax.axis_index("seq"), lax.axis_index("grp")
    chip, core = s // 2, s % 2
    sent = []

    def at(s2, g2):
        return {"seq": s2, "grp": g2}

    def turn(i, k, n):
        return lax.rem(i + k, n)

    def remote(src, dst, ss, rs, to):
        return pltpu.make_async_remote_copy(
            src_ref=src, dst_ref=dst, send_sem=ss, recv_sem=rs, device_id=to, device_id_type=pl.DeviceIdType.MESH
        )

    def go(copies):
        for c in copies:
            c.start()
        sent.extend(copies)

    def landed(copies):
        for c in copies:
            c.wait_recv()

    left, right = turn(s, z.n_seq - 1, z.n_seq), turn(s, 1, z.n_seq)
    sibling = chip * 2 + (1 - core)
    across = turn(s, z.n_seq - 1 + 2 * core, z.n_seq)

    def chip_peer(k):
        return at(turn(chip, k, z.n_chip) * 2 + core, g)

    def grp_peer(k):
        return at(s, turn(g, k, z.n_grp))

    barrier = pltpu.get_barrier_semaphore()
    peers = [at(sibling, g), at(across, g)]
    peers += [chip_peer(k) for k in range(1, z.n_chip)] + [grp_peer(k) for k in range(1, z.n_grp)]
    for to in peers:
        pl.semaphore_signal(barrier, inc=1, device_id=to, device_id_type=pl.DeviceIdType.MESH)

    def tap_place(q):
        part, q = divmod(q, z.gpp * z.n_seq)
        return part, q // z.gpp, (q % z.gpp) * 16

    for q in range(TAPS * z.gpt):
        j, r = q // z.gpt, (q % z.gpt) * 16
        h = min(16, z.cs - r)
        part, piece, o = tap_place(q)
        m["wbuf"][part, 0, piece // 2, piece % 2, o : o + h, :] = conv_ref[j, r : r + h, :]
    for q in range(z.gpt):
        r = q * 16
        h = min(16, z.cs - r)
        piece, o = q // z.ppp, (q % z.ppp) * 16
        m["pbuf"][0, piece // 2, piece % 2, o : o + h, :] = proj_ref[r : r + h, :]
    m["seg"][EDGE : EDGE + z.rows, :] = jnp.broadcast_to(seg_ref[...], (128, z.rows)).T

    pl.semaphore_wait(barrier, len(peers))

    def gather_c(i, buf):
        return [
            remote(buf.at[0, chip, core], buf.at[k, chip, core], m["gc_s"].at[i, k], m["gc_r"].at[i, k], grp_peer(k))
            for k in range(1, z.n_grp)
        ]

    def gather_b(i, buf):
        part = buf.at[pl.ds(1, z.n_grp - 1), chip, core]
        return [
            remote(part, part, m["gb_s"].at[i, k], m["gb_r"].at[i, k], chip_peer(k)) for k in range(1, z.n_chip)
        ]

    def gather_a(i, buf):
        part = buf.at[pl.ds(1, z.n_grp - 1), :, core]
        return [remote(part, part, m["ga_s"].at[i], m["ga_r"].at[i], at(sibling, g))]

    go(pc := gather_c(0, m["pbuf"]))
    taps_buf = [m["wbuf"].at[i] for i in range(z.parts)]
    wc = [gather_c(1 + i, buf) for i, buf in enumerate(taps_buf)]
    wb, wa = [None] * z.parts, [None] * z.parts
    for copies in wc:
        go(copies)

    halos = []
    ends = (pl.ds(0, EDGE), pl.ds(z.rows - EDGE, EDGE))
    seg_ends = (pl.ds(EDGE, EDGE), pl.ds(z.rows, EDGE))
    for i, (src, dst, cuts) in enumerate(
        ((x_ref, m["xh"], ends), (m["seg"], m["sh"], seg_ends))
    ):
        for side, to in ((1, left), (0, right)):
            halos.append(remote(
                src.at[cuts[1 - side]], dst.at[side], m["halo_s"].at[2 * i + side], m["halo_r"].at[2 * i + side], at(to, g)
            ))
    go(halos)
    def act_rows(first, count):
        def step(t, _):
            b = pl.multiple_of(t * 32, 32)
            r, _inv = normalised(x_ref[pl.ds(b, 32), :].astype(F32))
            cdf = gate(r)
            m["act"][pl.ds(EDGE + b, 32), :] = (r * cdf).astype(BF16).astype(F32)
            m["slope"][pl.ds(b, 32), :] = cdf + r * (jnp.exp(-0.5 * r * r) * (1.0 / math.sqrt(2.0 * math.pi)))
            return 0

        lax.fori_loop(first // 32, (first + count) // 32, step, 0, unroll=4)

    def forward_b(i):
        if i < z.parts:
            landed(wc[i])
            wb[i] = gather_b(1 + i, taps_buf[i])
            go(wb[i])

    def forward_a(i):
        if i < z.parts:
            landed(wb[i])
            wa[i] = gather_a(1 + i, taps_buf[i])
            go(wa[i])

    half = z.rows // 2
    act_rows(0, half)
    landed(pc)
    go(pb := gather_b(0, m["pbuf"]))
    act_rows(half, half)
    forward_b(0)

    landed(halos)
    for side, where in ((0, 0), (1, EDGE + z.rows)):
        r, _inv = normalised(m["xh"][side].astype(F32))
        m["act"][where : where + EDGE, :] = (r * gate(r)).astype(BF16).astype(F32)
        outside = (s == 0) if side == 0 else (s == z.n_seq - 1)
        m["seg"][where : where + EDGE, :] = jnp.where(outside, -1, m["sh"][side])

    def spread(src, part):
        def step(t, _):
            b = pl.multiple_of(t * 64, 64)
            seg = m["seg"][pl.ds(b, 64 + 2 * EDGE), :]
            own = seg[EDGE : EDGE + 64]
            masks = [seg[14 + j : 78 + j] == own for j in range(TAPS)]
            for o in range(0, z.c0, 128):
                window = src[pl.ds(b, 64 + 2 * EDGE), o : o + 128]
                for j in range(TAPS):
                    cut = jnp.where(masks[j], window[14 + j : 78 + j], 0.0).astype(BF16)
                    m["shifted"][pl.ds(b, 64), j * z.c0 + o : j * z.c0 + o + 128] = cut
            return 0

        n = z.rows // 128
        lax.fori_loop(part * n, part * n + n, step, 0, unroll=4)

    spread(m["act"], 0)
    forward_b(1)
    landed(pb)
    go(pa := gather_a(0, m["pbuf"]))
    spread(m["act"], 1)
    forward_b(2)

    landed(pa)
    for k in range(z.n_grp):
        base = lax.rem(g + z.n_grp - k, z.n_grp) * z.cs
        for q in range(z.gpt):
            r = q * 16
            h = min(16, z.cs - r)
            piece, o = q // z.ppp, (q % z.ppp) * 16
            rows = m["pbuf"][k, piece // 2, piece % 2, o : o + h, :].astype(z.stage)
            m["pf"][pl.ds(pl.multiple_of(base + r, math.gcd(z.cs, 16)), h), :] = rows
    proj = m["pf"][...].astype(BF16)

    pool_grad = (dot(proj, cot_ref[...]) * 0.5).astype(BF16)
    double = pick(256, 128, 0, 2)
    double_t = double.T.astype(BF16)
    double = double.astype(BF16)
    for t in range(z.half // 128):
        block = pool_grad[:, t * 128 : t * 128 + 128]
        m["grad"][EDGE + t * 256 : EDGE + t * 256 + 256, :] = dot(double, block, NT)
        m["gradt"][:, t * 256 : t * 256 + 256] = dot(block, double_t).astype(BF16)
    edges = []
    for i, (src, dst, to) in enumerate(((EDGE, EDGE + z.rows, left), (EDGE + z.rows - 8, EDGE - 8, right))):
        edges.append(remote(
            m["grad"].at[pl.ds(src, 8)], m["grad"].at[pl.ds(dst, 8)], m["halo_s"].at[4 + i], m["halo_r"].at[4 + i], at(to, g)
        ))
    go(edges)
    proj_t = proj.T

    forward_b(3)
    forward_a(0)

    def unit(u):
        return ("c", u, z.dc) if u < TAPS else ("p", 0, z.dp)

    live = {}

    def reduce_a(u, term):
        n, i, d = unit(u)
        acc = m[n + "_acc"]
        for b in range(z.n_seq):
            acc[i, b // 2, b % 2, 0:d, :] = term[b * d : b * d + d]
        for q in range(z.n_chip):
            m[n + "_sa"][i, q] = acc[i, q, 1 - core].astype(BF16)
        go(c := [remote(m[n + "_sa"].at[i], m[n + "_ra"].at[i], m["ra_s"].at[u], m["ra_r"].at[u], at(sibling, g))])
        live["a", u] = c

    def reduce_b(u):
        n, i, d = unit(u)
        landed(live["a", u])
        for q in range(z.n_chip):
            m[n + "_kb"][i, q] = m[n + "_acc"][i, q, core] + m[n + "_ra"][i, q].astype(F32)
        copies = []
        for k in range(1, z.n_chip):
            m[n + "_sb"][i, k] = m[n + "_kb"][i, turn(chip, k, z.n_chip)].astype(BF16)
            copies.append(remote(
                m[n + "_sb"].at[i, k], m[n + "_rb"].at[i, k], m["rb_s"].at[u, k], m["rb_r"].at[u, k], chip_peer(k)
            ))
        go(copies)
        live["b", u] = copies

    def reduce_c(u):
        n, i, d = unit(u)
        landed(live["b", u])
        total = m[n + "_kb"][i, chip]
        for k in range(1, z.n_chip):
            total = total + m[n + "_rb"][i, k].astype(F32)
        lanes = z.c0 // z.n_grp
        for k in range(z.n_grp):
            m[n + "_kc"][i, k] = total[:, k * lanes : k * lanes + lanes]
        copies = []
        for k in range(1, z.n_grp):
            m[n + "_sc"][i, k] = m[n + "_kc"][i, turn(g, k, z.n_grp)].astype(BF16)
            copies.append(remote(
                m[n + "_sc"].at[i, k], m[n + "_rc"].at[i, k], m["rc_s"].at[u, k], m["rc_r"].at[u, k], grp_peer(k)
            ))
        go(copies)
        live["c", u] = copies

    def reduce_end(u):
        n, i, d = unit(u)
        landed(live["c", u])
        total = m[n + "_kc"][i, g]
        for k in range(1, z.n_grp):
            total = total + m[n + "_rc"][i, k].astype(F32)
        if u < TAPS:
            cg_ref[u] = total[0:d]
        else:
            pg_ref[...] = total[0:d]

    for j in range(TAPS):
        reduce_a(j, dot(m["gradt"][...], m["shifted"][:, j * z.c0 : j * z.c0 + z.c0]))
        if j == 1:
            forward_a(1)
        if j == 3:
            forward_a(2)

    def assemble(i):
        if i >= z.parts:
            return
        landed(wa[i])
        for k in range(z.n_grp):
            base = lax.rem(g + z.n_grp - k, z.n_grp) * z.cs
            for q in range(TAPS * z.gpt):
                part, piece, o = tap_place(q)
                if part != i:
                    continue
                j, r = q // z.gpt, (q % z.gpt) * 16
                h = min(16, z.cs - r)
                rows = m["wbuf"][part, k, piece // 2, piece % 2, o : o + h, :].astype(z.stage)
                place = pl.multiple_of(base + r, math.gcd(z.cs, 16))
                m["wf"][pl.ds(j * z.c0 + place, h), :] = rows
                m["wb"][pl.ds(place, h), (TAPS - 1 - j) * z.c0 : (TAPS - j) * z.c0] = rows

    reduce_b(0)
    assemble(0)
    assemble(1)
    reduce_b(1)
    forward_a(3)
    reduce_b(2)
    assemble(2)
    reduce_b(3)
    reduce_b(4)
    assemble(3)

    halve = (pick(256, 128, 0, 2).T * 0.5).astype(BF16)
    for t in range(z.rows // 256):
        a = t * 256
        conv = dot(m["shifted"][a : a + 256, :], m["wf"][...].astype(BF16))
        hidden = (x_ref[a : a + 256, :].astype(F32) + conv).astype(BF16)
        m["pooled"][a // 2 : a // 2 + 128, :] = dot(halve, hidden).astype(BF16)
    pooled = m["pooled"][...]
    reduce_a(TAPS, dot(cot_ref[...], pooled))
    po_ref[...] = dot(proj_t, pooled, NT).astype(BF16)

    landed(edges)
    reduce_b(TAPS)
    reduce_c(0)
    spread(m["grad"], 0)
    reduce_c(1)
    reduce_c(2)
    spread(m["grad"], 1)

    def last(t, _):
        b = pl.multiple_of(t * 32, 32)
        r, inverse = normalised(x_ref[pl.ds(b, 32), :].astype(F32))
        ng = m["act"][pl.ds(b, 32), :]
        centred = ng - r * jnp.mean(ng * r, axis=-1, keepdims=True)
        ig_ref[pl.ds(b, 32), :] = (m["grad"][pl.ds(EDGE + b, 32), :] + centred * inverse).astype(BF16)
        return 0

    for t in range(z.rows // 256):
        a = t * 256
        act_grad = dot(m["shifted"][a : a + 256, :], m["wb"][...].astype(BF16), NT)
        m["act"][a : a + 256, :] = act_grad * m["slope"][a : a + 256, :]
        if t == 0:
            reduce_c(3)
        if t == 1:
            reduce_c(4)
        if t == 2:
            reduce_c(TAPS)
        lax.fori_loop(a // 32, a // 32 + 8, last, 0, unroll=8)
    for u in range(TAPS + 1):
        reduce_end(u)
    for c in sent:
        c.wait_send()


def finish(*refs):
    ins, outs, held, came, left = refs[:4], refs[4:8], refs[8:12], refs[12], refs[13]
    first = [pltpu.make_async_copy(a, b, came.at[i]) for i, (a, b) in enumerate(zip(ins, held))]
    then = [pltpu.make_async_copy(a, b, left.at[i]) for i, (a, b) in enumerate(zip(held, outs))]
    for c in first:
        c.start()
    for c, d in zip(first, then):
        c.wait()
        d.start()
    for d in then:
        d.wait()


def body(mesh, inputs, segment, conv_weight, proj_weight, cotangent):
    z = Sizes(mesh, inputs.shape[1:], conv_weight.shape, proj_weight.shape, cotangent.shape[:0:-1])
    shapes = scratch(z)
    vmem = pl.BlockSpec(memory_space=pltpu.VMEM)
    lanes = z.c0 // z.n_grp
    po, ig, cg, pg = pl.pallas_call(
        functools.partial(kernel, z, tuple(shapes)),
        out_shape=(
            jax.ShapeDtypeStruct((z.c1, z.half), BF16),
            jax.ShapeDtypeStruct((z.rows, z.c0), BF16),
            jax.ShapeDtypeStruct((TAPS, z.dc, lanes), F32),
            jax.ShapeDtypeStruct((z.dp, lanes), F32),
        ),
        in_specs=[vmem] * 5,
        out_specs=[vmem] * 4,
        scratch_shapes=list(shapes.values()),
        compiler_params=pltpu.CompilerParams(
            collective_id=0, has_side_effects=True, vmem_limit_bytes=56 * 1024 * 1024
        ),
    )(inputs[0], segment, conv_weight, proj_weight, cotangent[0].T)
    outs = (po, ig, cg, pg)
    po, ig, cg, pg = pl.pallas_call(
        finish,
        out_shape=tuple(jax.ShapeDtypeStruct(o.shape, o.dtype) for o in outs),
        in_specs=[pl.BlockSpec(memory_space=pl.ANY)] * 4,
        out_specs=[pl.BlockSpec(memory_space=pl.ANY)] * 4,
        scratch_shapes=[pltpu.VMEM(o.shape, o.dtype) for o in outs] + [pltpu.SemaphoreType.DMA((4,))] * 2,
        compiler_params=pltpu.CompilerParams(vmem_limit_bytes=56 * 1024 * 1024),
    )(*outs)
    return po.T[None], ig[None], jnp.swapaxes(cg, 1, 2), pg.T


def solution(mesh):
    return jax.shard_map(
        functools.partial(body, mesh),
        mesh=mesh,
        in_specs=(
            P("grp", "seq", None),
            P("grp", "seq"),
            P(None, "grp", None),
            P("grp", None),
            P("grp", "seq", None),
        ),
        out_specs=(
            P("grp", "seq", None),
            P("grp", "seq", None),
            P(None, "grp", "seq"),
            P("grp", "seq"),
        ),
        check_vma=False,
    )
```
